32 devices in a mesh: row: 8 (over z, core), col: 4 (over y, x).
Axes of the slice: x: 2, y: 2, z: 4, core: 2. Of those that a mesh axis runs over, the one named last changes fastest.
Arguments:
- gbar: float32 [16, 1024, 32, 512], P(None, 'row', None, 'col'), as said below
- panel: float32 [32, 512, 256], P(None, ('col', 'row')), may hold values from -0.046875 to 0.046875
- panel_adj: float32 [16, 1024, 256], P(None, ('row', 'col')), may hold values from -6 to 6
- factor: float32 [256, 256], replicated, as said below
- factor_adj: float32 [256, 256], replicated, may hold values from -6 to 6
Outputs:
- lower_adj: float32 [16, 1024, 256], P(None, ('row', 'col'))
- corner_adj: float32 [256, 256], replicated
The draws below stay inside these ranges and needn't reach their ends.
Inputs may be any that keep to these rules, and one draw needn't show every extreme that they name: gbar holds a symmetric 16384 x 16384 matrix. factor is lower triangular with a positive diagonal.
All inputs are finite; a program needn't handle non-finite values.
Results may differ from the reference program's by a relative error of at most 0.000075.
Values sent between devices are 32-bit elements; how exact they have to be, the bound alone decides.
A program may use at most 128 MiB of HBM per device.

```python
import jax
import jax.numpy as jnp
from jax import lax

N = 16384
B = 256
ROW_BLOCKS = 16
COL_BLOCKS = 32


def draw_gbar(key, part):
    first = jax.random.fold_in(key, 11)
    values = jax.random.normal(first, (N, N), jnp.float32)
    matrix = (values + values.T) * 0.35355339
    return matrix.reshape(ROW_BLOCKS, N // ROW_BLOCKS, COL_BLOCKS, N // COL_BLOCKS)


def draw_factor(key, part):
    first = jax.random.fold_in(key, 21)
    second = jax.random.fold_in(key, 22)
    diagonal = jax.random.uniform(first, (B,), jnp.float32, 1.5, 3.0)
    lower = jax.random.normal(second, (B, B), jnp.float32)
    lower = lower * (0.5 * B ** (-0.5))
    return jnp.tril(lower, -1) + jnp.diag(diagonal)


def levels(stream_key, shape, cuts, low, largest):
    gain = 1.0
    for position, blocks in cuts:
        draws = jax.random.uniform(jax.random.fold_in(jax.random.fold_in(stream_key, 6), position), (blocks,), jnp.float32, low / len(cuts), largest / len(cuts))
        gain = gain * jnp.repeat(jnp.exp(draws), shape[position] // blocks).reshape((-1,) + (1,) * (len(shape) - 1 - position))
    return gain


def centred(own_key, extent, scale, bound, shards=(), held_as=jnp.bfloat16):
    gain = levels(own_key, extent, shards, -0.22, 0.18) if shards else 1.0
    drawn = jax.random.normal(own_key, extent, jnp.float32) * scale * gain
    return jnp.minimum(jnp.maximum(drawn, -bound), bound).astype(held_as)


def setup_inputs(seed: int = 0) -> dict:
    streams_of = jax.random.split(jax.random.key(seed), 6)
    gbar = draw_gbar(jax.random.fold_in(streams_of[5], 71), 0)
    panel = centred(streams_of[1], (COL_BLOCKS, N // COL_BLOCKS, B), N ** -0.5, 0.046875, ((1, 32),), jnp.float32)
    panel_adj = centred(streams_of[2], (ROW_BLOCKS, N // ROW_BLOCKS, B), 1.0, 6.0, ((1, 32),), jnp.float32)
    factor = draw_factor(jax.random.fold_in(streams_of[5], 71), 0)
    factor_adj = centred(streams_of[4], (B, B), 1.0, 6.0, (), jnp.float32)
    return {"gbar": gbar, "panel": panel, "panel_adj": panel_adj, "factor": factor, "factor_adj": factor_adj}


def reference(gbar, panel, panel_adj, factor, factor_adj):
    highest = lax.Precision.HIGHEST
    matrix = gbar.reshape(N, N)
    columns = panel.reshape(N, B)
    adjoint = panel_adj.reshape(N, B)
    trailing = jnp.dot(matrix.astype(jnp.float32), columns.astype(jnp.float32), precision=highest, preferred_element_type=jnp.float32)
    panel_total = adjoint - 2.0 * trailing
    inverse = jax.scipy.linalg.solve_triangular(factor, jnp.eye(B, dtype=jnp.float32), lower=True)
    lower_full = jnp.dot(panel_total.astype(jnp.float32), inverse.astype(jnp.float32), precision=highest, preferred_element_type=jnp.float32)
    diag_total = factor_adj - jnp.dot(lower_full.T.astype(jnp.float32), columns.astype(jnp.float32), precision=highest, preferred_element_type=jnp.float32)
    projected = jnp.dot(factor.T.astype(jnp.float32), diag_total.astype(jnp.float32), precision=highest, preferred_element_type=jnp.float32)
    halved = jnp.tril(projected) - 0.5 * jnp.diag(jnp.diag(projected))
    middle = jnp.dot(jnp.dot(inverse.T.astype(jnp.float32), halved.astype(jnp.float32), precision=highest, preferred_element_type=jnp.float32).astype(jnp.float32), inverse.astype(jnp.float32), precision=highest, preferred_element_type=jnp.float32)
    corner_adj = 0.5 * (middle + middle.T)
    return (lower_full.reshape(panel_adj.shape), corner_adj)
```

```python
import functools

import jax
import jax.numpy as jnp
from jax import lax
from jax.experimental import pallas as pl
from jax.experimental.pallas import tpu as pltpu
from jax.sharding import PartitionSpec as P


def broadcast(value, axis, source):
    kept = jnp.where(lax.axis_index(axis) == source, value, 0).astype(value.dtype)
    return lax.psum(kept, axis)


def corner_reduce(corner):
    return lax.psum(corner, ("row", "col"))


def plain_device(gbar, panel, panel_adj, factor, factor_adj):
    highest = lax.Precision.HIGHEST
    row_at = lax.axis_index("row")
    col_at = lax.axis_index("col")
    n_row = lax.axis_size("row")
    n_col = lax.axis_size("col")
    panel_width = factor.shape[0]
    row_share = panel_adj.shape[1]
    column = lax.all_gather(panel, "row", axis=1, tiled=True)
    product = jnp.einsum(
        "arcs,csk->ark", gbar, column, precision=highest, preferred_element_type=jnp.float32
    )
    spread = jnp.zeros(product.shape, jnp.float32)
    spread = lax.dynamic_update_slice_in_dim(spread, panel_adj, col_at * row_share, 1)
    partial_value = spread - 2.0 * product
    inverse = jax.scipy.linalg.solve_triangular(
        factor, jnp.eye(panel_width, dtype=jnp.float32), lower=True
    )
    stride_ratio = n_row // n_col
    blocks = column.shape[0] // stride_ratio
    local_rows = lax.dynamic_index_in_dim(
        column.reshape(blocks, stride_ratio, column.shape[1], panel_width),
        row_at // n_col,
        1,
        keepdims=False,
    )
    rows_here = broadcast(local_rows, "col", row_at % n_col)
    mine = lax.dynamic_slice_in_dim(rows_here, col_at * row_share, row_share, 1)
    summed = lax.psum(partial_value, "col")
    owned_part = lax.dynamic_slice_in_dim(summed, col_at * row_share, row_share, 1)
    owned_rows = jnp.einsum(
        "ark,kj->arj", owned_part, inverse, precision=highest, preferred_element_type=jnp.float32
    )
    corner = jnp.einsum(
        "ark,arj->kj", owned_rows, mine, precision=highest, preferred_element_type=jnp.float32
    )
    corner_total = corner_reduce(corner)
    adjusted = factor_adj - corner_total
    projected = jnp.dot(factor.T, adjusted, precision=highest, preferred_element_type=jnp.float32)
    halved = jnp.tril(projected) - 0.5 * jnp.diag(jnp.diag(projected))
    middle = jnp.dot(
        jnp.dot(inverse.T, halved, precision=highest, preferred_element_type=jnp.float32),
        inverse,
        precision=highest,
        preferred_element_type=jnp.float32,
    )
    return (owned_rows, 0.5 * (middle + middle.T))


HALVES = 2
PARTS = 2
TILES = 4
BASE = 32
MESH = pl.DeviceIdType.MESH


def exact(a, b, dims=((1,), (0,))):
    return lax.dot_general(
        a,
        b,
        (dims, ((), ())),
        precision=lax.Precision.HIGHEST,
        preferred_element_type=jnp.float32,
    )


def lower_inverse(factor):
    n = factor.shape[0]
    groups = n // BASE
    rows = lax.broadcasted_iota(jnp.int32, (n, n), 0)
    cols = lax.broadcasted_iota(jnp.int32, (n, n), 1)
    factor = jnp.where(rows >= cols, factor, 0.0)
    same = (rows // BASE) == (cols // BASE)
    at_row = lax.broadcasted_iota(jnp.int32, (n, 128), 0)
    at_col = lax.broadcasted_iota(jnp.int32, (n, 128), 1)
    pick = jnp.where(at_row % BASE == at_col, 1.0, 0.0).astype(jnp.float32)
    compact = exact(jnp.where(same, factor, 0.0), pick).reshape(groups, BASE, 128)
    solved = pick.reshape(groups, BASE, 128)
    inner = lax.broadcasted_iota(jnp.int32, (groups, BASE, 128), 1)
    for j in range(BASE):
        line = solved[:, j : j + 1, :] / compact[:, j : j + 1, j : j + 1]
        below = compact[:, :, j : j + 1] * line
        solved = jnp.where(inner == j, line, jnp.where(inner > j, solved - below, solved))
    full = jnp.where(same, exact(solved.reshape(n, 128), pick, ((1,), (1,))), 0.0)
    size = BASE
    while size < n:
        off = ((rows // (2 * size)) == (cols // (2 * size))) & ((rows // size) > (cols // size))
        cross = exact(exact(full, jnp.where(off, factor, 0.0)), full)
        full = full - cross
        size *= 2
    return full


def fused(
    n_row, n_col,
    gbar, panel, panel_adj, factor, factor_adj,
    owned_out, corner_out,
    stage, high, low, gathered, right, acc, parts_in, mine, inverse_ref, part, mids, mid, smalls, total,
    stage_sem, own_sem, z_send, z_recv, sib_send, sib_recv, fwd_send, fwd_recv,
    rs_send, rs_recv, mine_send, mine_recv, a_send, a_recv, b_send, b_recv, c_send, c_recv, d_send, d_recv,
):
    row = lax.axis_index("row")
    col = lax.axis_index("col")
    nz = n_row // 2
    z = row // 2
    core = row % 2
    blocks, height = panel_adj.shape[0], panel_adj.shape[1]
    groups = 2 * panel.shape[0]
    share = panel.shape[2]
    width = factor.shape[0]
    half_width = width // HALVES
    per_part = groups // PARTS
    tall = n_col * height
    depth = n_row * share

    def z_row(d, c):
        return lax.rem(z + d + nz, nz) * 2 + c

    sibling = z * 2 + 1 - core

    def load(b, slot):
        return pltpu.make_async_copy(gbar.at[b], stage.at[slot], stage_sem.at[slot])

    load(0, 0).start()
    load(1, 1).start()

    items = [(h, j) for h in range(HALVES) for j in range(PARTS)]

    def slot_of(q, source):
        h, j = items[q]
        half = per_part // 2
        return gathered.at[h, pl.ds(j * half, half), :, source]

    def remote(src, dst, ssem, rsem, r, c):
        return pltpu.make_async_remote_copy(
            src_ref=src, dst_ref=dst, send_sem=ssem, recv_sem=rsem, device_id=(r, c), device_id_type=MESH
        )

    def flat(h, j):
        half = per_part // 2
        return panel.at[pl.ds(j * half, half), :, :, pl.ds(h * half_width, half_width)]

    def z_copy(q, d):
        return remote(flat(*items[q]), slot_of(q, row), z_send.at[q, d - 1], z_recv.at[q, d - 1], z_row(d, core), col)

    def sib_copy(q):
        return remote(flat(*items[q]), slot_of(q, row), sib_send.at[q], sib_recv.at[q], sibling, col)

    def fwd_copy(q, d):
        source = z_row(-d, core)
        return remote(
            slot_of(q, source), slot_of(q, source), fwd_send.at[q, d - 1], fwd_recv.at[q, d - 1], sibling, col
        )

    def own_copy(q):
        return pltpu.make_async_copy(flat(*items[q]), slot_of(q, row), own_sem.at[q])

    for q in range(len(items)):
        for d in range(1, nz):
            z_copy(q, d).start()
        sib_copy(q).start()
        own_copy(q).start()

    def prepare(pair, carry):
        for slot in range(2):
            b = pair * 2 + slot
            load(b, slot).wait()
            for c in range(groups):
                value = stage[slot, pl.ds(c, tall, stride=groups), :]
                top = value.astype(jnp.bfloat16)
                rest = (value - top.astype(jnp.float32)).astype(jnp.bfloat16)
                at = pl.ds(pl.multiple_of(b * tall, tall), tall)
                high[at, c * depth : (c + 1) * depth] = top
                low[at, c * depth : (c + 1) * depth] = rest

            @pl.when(b + 2 < blocks)
            def _():
                load(b + 2, slot).start()

        return carry

    lax.fori_loop(0, blocks // 2, prepare, 0)
    inverse_ref[...] = lower_inverse(factor[...])

    tile_blocks = blocks // TILES
    tile_rows = tile_blocks * tall

    def rs_copy(h, d, m):
        peer = lax.rem(col + d, n_col)
        at = pl.ds(m * tile_blocks, tile_blocks)
        return remote(
            acc.at[h, at, pl.ds(pl.multiple_of(peer * height, height), height)],
            parts_in.at[d - 1, h, at],
            rs_send.at[h, d - 1, m],
            rs_recv.at[h, d - 1, m],
            row,
            peer,
        )

    def compute(q):
        h, j = items[q]
        own_copy(q).wait()
        sib_copy(q).wait_recv()
        for d in range(1, nz):
            fwd_copy(q, d).wait_recv()
        values = gathered[h, j * per_part // 2 : (j + 1) * per_part // 2].reshape(per_part * depth, half_width)
        top = values.astype(jnp.bfloat16)
        right[:, :half_width] = top
        right[:, half_width:] = (values - top.astype(jnp.float32)).astype(jnp.bfloat16)

        def tile(m, carry):
            at = pl.ds(pl.multiple_of(m * tile_rows, tile_rows), tile_rows)
            span = pl.ds(j * per_part * depth, per_part * depth)
            both = jnp.dot(high[at, span], right[...], preferred_element_type=jnp.float32)
            small = jnp.dot(low[at, span], right[:, :half_width], preferred_element_type=jnp.float32)
            out = (both[:, :half_width] + (both[:, half_width:] + small)).reshape(tile_blocks, tall, half_width)
            where = pl.ds(m * tile_blocks, tile_blocks)
            if j == 0:
                acc[h, where] = out
            else:
                acc[h, where] += out
            if j == PARTS - 1:
                for d in range(1, n_col):
                    rs_copy(h, d, m).start()
            return carry

        lax.fori_loop(0, TILES, tile, 0)

    to_half = lax.rem(row, 2)

    def mine_dst():
        return mine.at[:, pl.ds(pl.multiple_of(to_half * share, share), share)]

    def mine_copy(p):
        return remote(panel.at[:, p], mine_dst(), mine_send.at[p], mine_recv.at[to_half], col + p * n_col, row // 2)

    def is_self(p):
        return (col + p * n_col == row) & (row // 2 == col)

    def mine_start(p):
        @pl.when(is_self(p))
        def _():
            pltpu.make_async_copy(panel.at[:, p], mine_dst(), mine_recv.at[to_half]).start()

        @pl.when(jnp.logical_not(is_self(p)))
        def _():
            mine_copy(p).start()

    for q in range(len(items) + 1):
        if q < len(items):
            for d in range(1, nz):
                z_copy(q, d).wait_recv()
                fwd_copy(q, d).start()
        if q == len(items) - 1:
            mine_start(0)
            mine_start(1)
        if q >= 1:
            compute(q - 1)

    at_mine = pl.ds(pl.multiple_of(col * height, height), height)
    pieces = []
    for h in range(HALVES):
        for d in range(1, n_col):
            for m in range(TILES):
                rs_copy(h, d, m).wait_recv()
        summed = acc[h, :, at_mine, :]
        for d in range(1, n_col):
            summed = summed + parts_in[d - 1, h]
        lanes = slice(h * half_width, (h + 1) * half_width)
        pieces.append((panel_adj[:, :, lanes] - 2.0 * summed).reshape(blocks * height, half_width))
    inverse = inverse_ref[...]
    owned = exact(jnp.concatenate(pieces, axis=1), inverse)
    owned_out[...] = owned.reshape(blocks, height, width)
    for p in range(2):
        pltpu.make_async_copy(
            panel.at[:, p], mine.at[:, pl.ds(p * share, share)], mine_recv.at[p]
        ).wait()
    part[...] = exact(owned.T, mine[...].reshape(blocks * height, width))

    big = width // n_col
    tiny = big // n_row

    def a_copy(d):
        peer = lax.rem(col + d, n_col)
        src = part.at[pl.ds(pl.multiple_of(peer * big, big), big)]
        return remote(src, mids.at[d - 1], a_send.at[d - 1], a_recv.at[d - 1], row, peer)

    def b_copy(d):
        peer = lax.rem(row + d, n_row)
        src = mid.at[pl.ds(pl.multiple_of(peer * tiny, tiny), tiny)]
        return remote(src, smalls.at[d - 1], b_send.at[d - 1], b_recv.at[d - 1], peer, col)

    def c_ref(r):
        return total.at[pl.ds(pl.multiple_of(col * big + r * tiny, tiny), tiny)]

    def c_copy(d):
        return remote(c_ref(row), c_ref(row), c_send.at[d - 1], c_recv.at[d - 1], lax.rem(row + d, n_row), col)

    def c_from(d):
        src = c_ref(lax.rem(row - d + n_row, n_row))
        return remote(src, src, c_send.at[d - 1], c_recv.at[d - 1], lax.rem(row + d, n_row), col)

    def d_ref(c):
        return total.at[pl.ds(pl.multiple_of(c * big, big), big)]

    def d_copy(d):
        return remote(d_ref(col), d_ref(col), d_send.at[d - 1], d_recv.at[d - 1], row, lax.rem(col + d, n_col))

    def d_from(d):
        src = d_ref(lax.rem(col - d + n_col, n_col))
        return remote(src, src, d_send.at[d - 1], d_recv.at[d - 1], row, lax.rem(col + d, n_col))

    for d in range(1, n_col):
        a_copy(d).start()
    summed = part[pl.ds(pl.multiple_of(col * big, big), big), :]
    for d in range(1, n_col):
        a_copy(d).wait_recv()
        summed = summed + mids[d - 1]
    mid[...] = summed
    for d in range(1, n_row):
        b_copy(d).start()
    summed = mid[pl.ds(pl.multiple_of(row * tiny, tiny), tiny), :]
    for d in range(1, n_row):
        b_copy(d).wait_recv()
        summed = summed + smalls[d - 1]
    total[pl.ds(pl.multiple_of(col * big + row * tiny, tiny), tiny), :] = summed
    for d in range(1, n_row):
        c_copy(d).start()
    for d in range(1, n_row):
        c_from(d).wait_recv()
    for d in range(1, n_col):
        d_copy(d).start()
    for d in range(1, n_col):
        d_from(d).wait_recv()

    adjusted = factor_adj[...] - total[...]
    projected = exact(factor[...].T, adjusted)
    rows = lax.broadcasted_iota(jnp.int32, (width, width), 0)
    cols = lax.broadcasted_iota(jnp.int32, (width, width), 1)
    halved = jnp.where(rows > cols, projected, jnp.where(rows == cols, 0.5 * projected, 0.0))
    middle = exact(exact(inverse.T, halved), inverse)
    corner_out[...] = 0.5 * (middle + middle.T)

    for q in range(len(items)):
        for d in range(1, nz):
            z_copy(q, d).wait_send()
            fwd_copy(q, d).wait_send()
        sib_copy(q).wait_send()
    for h in range(HALVES):
        for d in range(1, n_col):
            for m in range(TILES):
                rs_copy(h, d, m).wait_send()
    for p in range(2):
        @pl.when(jnp.logical_not(is_self(p)))
        def _(p=p):
            mine_copy(p).wait_send()
    for d in range(1, n_col):
        a_copy(d).wait_send()
        d_copy(d).wait_send()
    for d in range(1, n_row):
        b_copy(d).wait_send()
        c_copy(d).wait_send()


def fast_device(n_row, n_col, gbar, panel, panel_adj, factor, factor_adj):
    blocks, tall, groups, depth = gbar.shape
    share, width = panel.shape[1], panel.shape[2]
    height = panel_adj.shape[1]
    half_width = width // HALVES
    nz = n_row // 2
    items = HALVES * PARTS
    f32, bf16 = jnp.float32, jnp.bfloat16
    dma = pltpu.SemaphoreType.DMA
    vmem = pl.BlockSpec(memory_space=pltpu.VMEM)
    return pl.pallas_call(
        functools.partial(fused, n_row, n_col),
        out_shape=(
            jax.ShapeDtypeStruct(panel_adj.shape, f32),
            jax.ShapeDtypeStruct(factor.shape, f32),
        ),
        in_specs=[pl.BlockSpec(memory_space=pl.ANY)] + [vmem] * 4,
        out_specs=(vmem, vmem),
        scratch_shapes=[
            pltpu.VMEM((2, tall * groups, depth), f32),
            pltpu.VMEM((blocks * tall, groups * depth), bf16),
            pltpu.VMEM((blocks * tall, groups * depth), bf16),
            pltpu.VMEM((HALVES, groups // 2, 2, n_row, share, half_width), f32),
            pltpu.VMEM((groups // PARTS * depth, width), bf16),
            pltpu.VMEM((HALVES, blocks, tall, half_width), f32),
            pltpu.VMEM((n_col - 1, HALVES, blocks, height, half_width), f32),
            pltpu.VMEM((blocks, height, width), f32),
            pltpu.VMEM((width, width), f32),
            pltpu.VMEM((width, width), f32),
            pltpu.VMEM((n_col - 1, width // n_col, width), f32),
            pltpu.VMEM((width // n_col, width), f32),
            pltpu.VMEM((n_row - 1, width // n_col // n_row, width), f32),
            pltpu.VMEM((width, width), f32),
            dma((2,)),
            dma((items,)),
            dma((items, nz - 1)),
            dma((items, nz - 1)),
            dma((items,)),
            dma((items,)),
            dma((items, nz - 1)),
            dma((items, nz - 1)),
            dma((HALVES, n_col - 1, TILES)),
            dma((HALVES, n_col - 1, TILES)),
            dma((2,)),
            dma((2,)),
            dma((n_col - 1,)),
            dma((n_col - 1,)),
            dma((n_row - 1,)),
            dma((n_row - 1,)),
            dma((n_row - 1,)),
            dma((n_row - 1,)),
            dma((n_col - 1,)),
            dma((n_col - 1,)),
        ],
        compiler_params=pltpu.CompilerParams(
            has_side_effects=True, vmem_limit_bytes=60 * 1024 * 1024
        ),
    )(
        gbar.reshape(blocks, tall * groups, depth),
        panel.reshape(groups // 2, 2, share, width),
        panel_adj,
        factor,
        factor_adj,
    )


def per_device(gbar, panel, panel_adj, factor, factor_adj):
    n_row, n_col = lax.axis_size("row"), lax.axis_size("col")
    width = factor.shape[0]
    blocks, tall, groups, depth = gbar.shape
    fits = (
        n_row == 2 * n_col
        and groups == 2 * blocks
        and panel.shape[1] % 8 == 0
        and depth == 128
        and width == 256
        and blocks % TILES == 0
        and width % (8 * n_row * n_col) == 0
        and gbar.size * 4 <= 36 * 1024 * 1024
    )
    if fits:
        return fast_device(n_row, n_col, gbar, panel, panel_adj, factor, factor_adj)
    return plain_device(gbar, panel, panel_adj, factor, factor_adj)


def solution(mesh):
    return jax.shard_map(
        per_device,
        mesh=mesh,
        in_specs=(
            P(None, "row", None, "col"),
            P(None, ("col", "row"), None),
            P(None, ("row", "col"), None),
            P(),
            P(),
        ),
        out_specs=(P(None, ("row", "col"), None), P()),
        check_vma=False,
    )
```
